32 devices in a mesh: seq: 8 (over z, y), wt: 4 (over x, core).
Axes of the slice: x: 2, y: 2, z: 4, core: 2. Of those that a mesh axis runs over, the one named last changes fastest.
Arguments:
- activations: bfloat16 [16384, 1536], P('seq', 'wt'), may hold values from -6 to 6
- first_norm_scale: float32 [1536], P('wt'), may hold values from 0.1 to 1.9
- first_norm_shift: float32 [1536], P('wt'), may hold values from -0.5 to 0.5
- first_kernel_weight: bfloat16 [3, 1536, 1536], P(None, 'seq', 'wt'), may hold values from -0.09375 to 0.09375
- second_norm_scale: float32 [1536], P('wt'), may hold values from 0.1 to 1.9
- second_norm_shift: float32 [1536], P('wt'), may hold values from -0.5 to 0.5
- second_kernel_weight: bfloat16 [3, 1536, 1536], P(None, 'seq', 'wt'), may hold values from -0.09375 to 0.09375
Outputs:
- tower_out: bfloat16 [16384, 1536], P('seq', 'wt')
The draws below stay inside these ranges and needn't reach their ends.
All inputs are finite; a program needn't handle non-finite values.
Results may differ from the reference program's by a relative error of at most 0.008.
Values may be sent and summed in bfloat16 or wider, within the bound.
A program may use at most 64 MiB of HBM per device.

```python
import jax
import jax.numpy as jnp

C = 1536
DILATION_FIRST = 256
DILATION_SECOND = 512
LENGTH = 16384


def block_scale(rng, extent, pieces, smallest, largest):
    gain = 1.0
    for dim, parts in pieces:
        steps = jax.random.uniform(jax.random.fold_in(jax.random.fold_in(rng, 6), dim), (parts,), jnp.float32, smallest / len(pieces), largest / len(pieces))
        gain = gain * jnp.repeat(jnp.exp(steps), extent[dim] // parts).reshape((-1,) + (1,) * (len(extent) - 1 - dim))
    return gain


def scatter_about(key, dims, deviation, limit, cuts=(), dtype=jnp.bfloat16):
    gain = block_scale(key, dims, cuts, -0.22, 0.18) if cuts else 1.0
    entries = jax.random.normal(key, dims, jnp.float32) * deviation * gain
    return jnp.minimum(jnp.maximum(entries, -limit), limit).astype(dtype)


def setup_inputs(seed: int = 0) -> dict:
    keys = jax.random.split(jax.random.key(seed), 8)
    return {
        "activations": scatter_about(keys[0], (LENGTH, C), 1.0, 6.0, ((0, 8), (1, 4))),
        "first_norm_scale": jnp.clip(1.0 + 0.18 * jax.random.normal(keys[1], (C,), jnp.float32), 0.1, 1.9),
        "first_norm_shift": jnp.clip(jax.random.uniform(keys[2], (C,), jnp.float32, -0.5, 0.5) * block_scale(keys[2], (C,), ((0, 4),), -0.4, 0.0), -0.5, 0.5),
        "first_kernel_weight": scatter_about(keys[3], (3, C, C), (3 * C) ** -0.5, 0.09375, ((1, 8), (2, 4))),
        "second_norm_scale": jnp.clip(1.0 + 0.18 * jax.random.normal(keys[4], (C,), jnp.float32), 0.1, 1.9),
        "second_norm_shift": jnp.clip(jax.random.uniform(keys[5], (C,), jnp.float32, -0.5, 0.5) * block_scale(keys[5], (C,), ((0, 4),), -0.4, 0.0), -0.5, 0.5),
        "second_kernel_weight": scatter_about(keys[6], (3, C, C), (3 * C) ** -0.5, 0.09375, ((1, 8), (2, 4))),
    }


def single_conv_layer(state, scale, shift, weight, reach):
    value = state.astype(jnp.float32) * scale[None, :] + shift[None, :]
    hidden = jax.nn.gelu(value, approximate=True).astype(jnp.bfloat16)
    total_rows = hidden.shape[0]
    padded = jnp.pad(hidden, ((reach, reach), (0, 0)))
    total = jnp.zeros((total_rows, hidden.shape[1]), jnp.float32)
    for tap in range(3):
        total = total + jnp.dot(padded[tap * reach:tap * reach + total_rows], weight[tap], preferred_element_type=jnp.float32)
    return (state.astype(jnp.float32) + total).astype(jnp.bfloat16)


def reference(activations, first_norm_scale, first_norm_shift, first_kernel_weight, second_norm_scale, second_norm_shift, second_kernel_weight):
    first_conv_layer = single_conv_layer(activations, first_norm_scale, first_norm_shift, first_kernel_weight, DILATION_FIRST)
    return single_conv_layer(first_conv_layer, second_norm_scale, second_norm_shift, second_kernel_weight, DILATION_SECOND)
```

```python
import functools

import jax
import jax.numpy as jnp
from jax import lax
from jax.experimental import pallas as pl
from jax.experimental.pallas import tpu as pltpu
from jax.sharding import PartitionSpec as P

DILATION_FIRST = 256
DILATION_SECOND = 512
CHUNK = 256
TAPS = 3


def tower_kernel(
    n, m, x_ref, s1_ref, b1_ref, w1_ref, s2_ref, b2_ref, w2_ref, out_ref,
    hid1, hid2, wb, one,
    s_p, r_p, s_q, r_q, s_y, r_y, s_x, r_x, s_c, r_c, s_f, r_f, s_h, r_h,
):
    s = lax.axis_index("seq")
    w = lax.axis_index("wt")
    lines = n // 2
    z, y = s // 2, lax.rem(s, 2)
    x_peer = lax.rem(w + m // 2, m)
    c_peer = w + 1 - 2 * lax.rem(w, 2)
    xc_peer = lax.rem(c_peer + m // 2, m)
    y_peer = s + 1 - 2 * y
    rows, cols = x_ref.shape
    kr = w1_ref.shape[1]
    nc = rows // CHUNK
    reach = (DILATION_FIRST // CHUNK, DILATION_SECOND // CHUNK)
    hids = (hid1, hid2)
    scales = (s1_ref, s2_ref)
    shifts = (b1_ref, b2_ref)
    has_prev, has_next = s > 0, s < n - 1
    up, down = z < lines - 1, z > 0
    steps = ((1, up), (-1, down))

    def rdma(src, dst, ss, rs, ds, dw):
        return pltpu.make_async_remote_copy(
            src_ref=src, dst_ref=dst, send_sem=ss, recv_sem=rs,
            device_id=(ds, dw), device_id_type=pl.DeviceIdType.MESH,
        )

    def span(e):
        return pl.ds(pl.multiple_of(e * CHUNK, CHUNK), CHUNK)

    def lane(j):
        return pl.ds(pl.multiple_of(j * cols, cols), cols)

    def krows(zz, yy):
        return pl.ds(pl.multiple_of((zz * 2 + yy) * kr, kr), kr)

    def msg_p(l, zz, d):
        ref = wb.at[l, :, krows(zz, y), :]
        i = 0 if d > 0 else 1
        return rdma(ref, ref, s_p.at[i, l, zz], r_p.at[l, zz], s + 2 * d, w)

    def msg_q(l, zz, d):
        ref = wb.at[l, pl.ds(TAPS - 1, 1), krows(zz, 1 - y), :]
        i = 0 if d > 0 else 1
        return rdma(ref, ref, s_q.at[i, l, zz], r_q.at[l, zz], s + 2 * d, w)

    def msg_y(l, zz, yy, count):
        ref = wb.at[l, pl.ds(0, count), krows(zz, yy), :]
        return rdma(ref, ref, s_y.at[l, zz], r_y.at[l, zz], y_peer, w)

    def weights_start(l):
        for d, there in steps:
            @pl.when(there)
            def _():
                msg_p(l, z, d).start()
        msg_y(l, z, y, TAPS).start()

    def weights_pair(l):
        msg_y(l, z, 1 - y, TAPS).wait_recv()
        for d, there in steps:
            @pl.when(there)
            def _():
                msg_q(l, z, d).start()

    def weights_step(l, k):
        for d, there in steps:
            zz = z - d * k
            onward = there

            @pl.when(jnp.logical_and(zz >= 0, zz < lines))
            def _():
                msg_p(l, zz, d).wait_recv()

                @pl.when(onward)
                def _():
                    msg_p(l, zz, d).start()

                msg_y(l, zz, y, TAPS - 1).start()
                msg_q(l, zz, d).wait_recv()

                @pl.when(onward)
                def _():
                    msg_q(l, zz, d).start()

    def weights_finish(l):
        for k in range(1, lines):
            for d in (1, -1):
                zz = z - d * k

                @pl.when(jnp.logical_and(zz >= 0, zz < lines))
                def _():
                    msg_y(l, zz, 1 - y, TAPS - 1).wait_recv()

    def weights_drain(l):
        msg_y(l, z, y, TAPS).wait_send()
        for k in range(lines):
            for d, there in steps:
                zz = z - d * k

                @pl.when(jnp.logical_and(zz >= 0, zz < lines))
                def _():
                    if k:
                        msg_y(l, zz, y, TAPS - 1).wait_send()

                    @pl.when(there)
                    def _():
                        msg_p(l, zz, d).wait_send()
                        msg_q(l, zz, d).wait_send()

    def msg_x(l, e, j):
        ref = hids[l].at[span(e), lane(j)]
        return rdma(ref, ref, s_x.at[l, e], r_x.at[l, e], s, x_peer)

    def msg_c(l, e, j):
        ref = hids[l].at[span(e), lane(j)]
        return rdma(ref, ref, s_c.at[l, e], r_c.at[l, e], s, c_peer)

    def msg_f(l, e, j):
        ref = hids[l].at[span(e), lane(j)]
        return rdma(ref, ref, s_f.at[l, e], r_f.at[l, e], s, c_peer)

    def msg_h(l, src, dst, d):
        hid = hids[l]
        return rdma(
            hid.at[span(src), lane(w)], hid.at[span(dst), lane(w)],
            s_h.at[l, dst], r_h.at[l, dst], s + d, w,
        )

    def emit(l, c, state):
        reach_l = reach[l]
        value = state.astype(jnp.float32) * scales[l][...] + shifts[l][...]
        hidden = jax.nn.gelu(value, approximate=True).astype(jnp.bfloat16)
        e = c + reach_l
        hids[l][span(e), lane(w)] = hidden

        @pl.when(jnp.logical_and(c < reach_l, has_prev))
        def _():
            msg_h(l, e, nc + e, -1).start()

        @pl.when(jnp.logical_and(c >= nc - reach_l, has_next))
        def _():
            msg_h(l, e, e - nc, 1).start()

        msg_x(l, e, w).start()
        msg_c(l, e, w).start()

    def halos(l):
        d = reach[l]
        return [(e, has_prev) for e in range(d)] + [
            (nc + d + e, has_next) for e in range(d)
        ]

    def halo_arrive(l, e, there):
        @pl.when(there)
        def _():
            msg_h(l, e, e, 1).wait_recv()
            msg_x(l, e, w).start()
            msg_c(l, e, w).start()

        @pl.when(jnp.logical_not(there))
        def _():
            hids[l][span(e), :] = jnp.zeros((CHUNK, m * cols), jnp.bfloat16)

    def forward(l, e, there=None):
        def go():
            msg_x(l, e, x_peer).wait_recv()
            msg_f(l, e, x_peer).start()

        if there is None:
            go()
        else:
            pl.when(there)(go)

    def ready(l, e, there=None):
        def go():
            msg_c(l, e, c_peer).wait_recv()
            msg_f(l, e, xc_peer).wait_recv()

        if there is None:
            go()
        else:
            pl.when(there)(go)

    def sent(l):
        d = reach[l]

        def one_chunk(e):
            msg_x(l, e, w).wait_send()
            msg_c(l, e, w).wait_send()
            msg_f(l, e, x_peer).wait_send()

        for e, there in halos(l):
            @pl.when(there)
            def _():
                one_chunk(e)
        for e in range(d, nc + d):
            one_chunk(e)
        for e in range(d):
            @pl.when(has_prev)
            def _():
                msg_h(l, d + e, nc + d + e, -1).wait_send()

            @pl.when(has_next)
            def _():
                msg_h(l, nc + e, e, 1).wait_send()

    def own_order(l):
        d = reach[l]
        return [(i + nc - d) % nc + d for i in range(nc)]

    def conv(l, c, state):
        d = reach[l]
        total = jnp.zeros((CHUNK, cols), jnp.float32)
        for tap in range(TAPS):
            total = total + jnp.dot(
                hids[l][span(c + tap * d), :], wb[l, tap],
                preferred_element_type=jnp.float32,
            )
        return (state.astype(jnp.float32) + total).astype(jnp.bfloat16)

    barrier = pltpu.get_barrier_semaphore()
    peers = [
        (True, y_peer, w), (True, s, x_peer), (True, s, c_peer),
        (up, s + 2, w), (down, s - 2, w), (has_next, s + 1, w), (has_prev, s - 1, w),
    ]
    expected = 3
    for there, ds, dw in peers:
        def greet(ds=ds, dw=dw):
            pl.semaphore_signal(
                barrier, inc=1, device_id=(ds, dw), device_id_type=pl.DeviceIdType.MESH
            )

        if there is True:
            greet()
        else:
            pl.when(there)(greet)
            expected = expected + there.astype(jnp.int32)
    wb[0, :, krows(z, y), :] = w1_ref[...]
    wb[1, :, krows(z, y), :] = w2_ref[...]
    pl.semaphore_wait(barrier, expected)

    weights_start(0)

    @pl.loop(0, nc)
    def _(i):
        c = lax.rem(i + nc - reach[0], nc)
        emit(0, c, x_ref[span(c), :])

    for e, there in halos(0):
        halo_arrive(0, e, there)
    weights_pair(0)
    k = 1
    incoming = [(e, None) for e in own_order(0)] + halos(0)
    for i, (e, there) in enumerate(incoming):
        forward(0, e, there)
        if i % 3 == 1 and k < lines:
            weights_step(0, k)
            k += 1
    for k in range(k, lines):
        weights_step(0, k)
    weights_start(1)
    weights_finish(0)
    for e, there in incoming:
        ready(0, e, there)

    @pl.loop(0, nc)
    def _(i):
        c = lax.rem(i + nc - reach[1], nc)
        state = conv(0, c, x_ref[span(c), :])
        one[span(c), :] = state
        emit(1, c, state)

    weights_pair(1)
    own, edge = own_order(1), halos(1)
    k = 1
    for i, e in enumerate(own):
        forward(1, e)
        if i >= 2 and i - 2 < len(edge):
            halo_arrive(1, *edge[i - 2])
        if i % 3 == 1 and k < lines:
            weights_step(1, k)
            k += 1
    for i in range(max(len(own) - 2, 0), len(edge)):
        halo_arrive(1, *edge[i])
    for k in range(k, lines):
        weights_step(1, k)
    for e, there in edge:
        forward(1, e, there)
    weights_finish(1)
    for e in own:
        ready(1, e)
    for e, there in edge:
        ready(1, e, there)

    @pl.loop(0, nc)
    def _(i):
        c = lax.rem(i + reach[1], nc)
        out_ref[span(c), :] = conv(1, c, one[span(c), :])

    for l in range(2):
        sent(l)
        weights_drain(l)


def shards(n, m, x, s1, b1, w1, s2, b2, w2):
    rows, cols = x.shape
    channels = m * cols
    lines = n // 2
    ext = rows // CHUNK + 2 * (DILATION_SECOND // CHUNK)
    dma = pltpu.SemaphoreType.DMA
    vmem = pl.BlockSpec(memory_space=pltpu.VMEM)
    return pl.pallas_call(
        functools.partial(tower_kernel, n, m),
        out_shape=jax.ShapeDtypeStruct((rows, cols), jnp.bfloat16),
        in_specs=[vmem] * 7,
        out_specs=vmem,
        scratch_shapes=[
            pltpu.VMEM((rows + 2 * DILATION_FIRST, channels), jnp.bfloat16),
            pltpu.VMEM((rows + 2 * DILATION_SECOND, channels), jnp.bfloat16),
            pltpu.VMEM((2, TAPS, channels, cols), jnp.bfloat16),
            pltpu.VMEM((rows, cols), jnp.bfloat16),
            dma((2, 2, lines)), dma((2, lines)),
            dma((2, 2, lines)), dma((2, lines)),
            dma((2, lines)), dma((2, lines)),
        ] + [dma((2, ext))] * 8,
        compiler_params=pltpu.CompilerParams(
            collective_id=0, has_side_effects=True, vmem_limit_bytes=56 * 1024 * 1024
        ),
        cost_estimate=pl.CostEstimate(
            flops=4 * TAPS * rows * channels * cols,
            bytes_accessed=4 * rows * cols + 4 * TAPS * w1.shape[1] * cols,
            transcendentals=2 * rows * cols,
        ),
    )(x, s1[None, :], b1[None, :], w1, s2[None, :], b2[None, :], w2)


def solution(mesh):
    placed = (
        P("seq", "wt"),
        P("wt"),
        P("wt"),
        P(None, "seq", "wt"),
        P("wt"),
        P("wt"),
        P(None, "seq", "wt"),
    )
    n, m = mesh.shape["seq"], mesh.shape["wt"]
    return jax.shard_map(
        functools.partial(shards, n, m), mesh=mesh, in_specs=placed,
        out_specs=P("seq", "wt"), check_vma=False,
    )
```

```python
import functools

import jax
import jax.numpy as jnp
from jax import lax
from jax.experimental import pallas as pl
from jax.experimental.pallas import tpu as pltpu
from jax.sharding import PartitionSpec as P

DILATION_FIRST = 256
DILATION_SECOND = 512
CHUNK = 256
TAPS = 3


def tower_kernel(
    n, m, x_ref, s1_ref, b1_ref, w1_ref, s2_ref, b2_ref, w2_ref, out_ref,
    hid1, hid2, wb, one, part_out, part_in, s_g, r_g,
    s_p, r_p, s_q, r_q, s_y, r_y, s_x, r_x, s_c, r_c, s_f, r_f, s_h, r_h,
):
    s = lax.axis_index("seq")
    w = lax.axis_index("wt")
    lines = n // 2
    z, y = s // 2, lax.rem(s, 2)
    x_peer = lax.rem(w + m // 2, m)
    c_peer = w + 1 - 2 * lax.rem(w, 2)
    xc_peer = lax.rem(c_peer + m // 2, m)
    y_peer = s + 1 - 2 * y
    rows, cols = x_ref.shape
    kr = w1_ref.shape[1]
    nc = rows // CHUNK
    reach = (DILATION_FIRST // CHUNK, DILATION_SECOND // CHUNK)
    edge = (0, reach[1])
    hids = (hid1, hid2)
    scales = (s1_ref, s2_ref)
    shifts = (b1_ref, b2_ref)
    has_prev, has_next = s > 0, s < n - 1
    up, down = z < lines - 1, z > 0
    steps = ((1, up), (-1, down))

    def rdma(src, dst, ss, rs, ds, dw):
        return pltpu.make_async_remote_copy(
            src_ref=src, dst_ref=dst, send_sem=ss, recv_sem=rs,
            device_id=(ds, dw), device_id_type=pl.DeviceIdType.MESH,
        )

    def span(e):
        return pl.ds(pl.multiple_of(e * CHUNK, CHUNK), CHUNK)

    def lane(j):
        return pl.ds(pl.multiple_of(j * cols, cols), cols)

    def krows(zz, yy):
        return pl.ds(pl.multiple_of((zz * 2 + yy) * kr, kr), kr)

    def msg_p(l, zz, d):
        ref = wb.at[l, :, krows(zz, y), :]
        i = 0 if d > 0 else 1
        return rdma(ref, ref, s_p.at[i, l, zz], r_p.at[l, zz], s + 2 * d, w)

    def msg_q(l, zz, d):
        ref = wb.at[l, pl.ds(TAPS - 1, 1), krows(zz, 1 - y), :]
        i = 0 if d > 0 else 1
        return rdma(ref, ref, s_q.at[i, l, zz], r_q.at[l, zz], s + 2 * d, w)

    def msg_y(l, zz, yy, count):
        ref = wb.at[l, pl.ds(0, count), krows(zz, yy), :]
        return rdma(ref, ref, s_y.at[l, zz], r_y.at[l, zz], y_peer, w)

    def weights_start(l):
        for d, there in steps:
            @pl.when(there)
            def _():
                msg_p(l, z, d).start()
        msg_y(l, z, y, TAPS).start()

    def weights_pair(l):
        msg_y(l, z, 1 - y, TAPS).wait_recv()
        for d, there in steps:
            @pl.when(there)
            def _():
                msg_q(l, z, d).start()

    def weights_step(l, k):
        for d, there in steps:
            zz = z - d * k
            onward = there

            @pl.when(jnp.logical_and(zz >= 0, zz < lines))
            def _():
                msg_p(l, zz, d).wait_recv()

                @pl.when(onward)
                def _():
                    msg_p(l, zz, d).start()

                msg_y(l, zz, y, TAPS - 1).start()
                msg_q(l, zz, d).wait_recv()

                @pl.when(onward)
                def _():
                    msg_q(l, zz, d).start()

    def weights_finish(l):
        for k in range(1, lines):
            for d in (1, -1):
                zz = z - d * k

                @pl.when(jnp.logical_and(zz >= 0, zz < lines))
                def _():
                    msg_y(l, zz, 1 - y, TAPS - 1).wait_recv()

    def weights_drain(l):
        msg_y(l, z, y, TAPS).wait_send()
        for k in range(lines):
            for d, there in steps:
                zz = z - d * k

                @pl.when(jnp.logical_and(zz >= 0, zz < lines))
                def _():
                    if k:
                        msg_y(l, zz, y, TAPS - 1).wait_send()

                    @pl.when(there)
                    def _():
                        msg_p(l, zz, d).wait_send()
                        msg_q(l, zz, d).wait_send()

    def msg_x(l, e, j):
        ref = hids[l].at[span(e), lane(j)]
        return rdma(ref, ref, s_x.at[l, e], r_x.at[l, e], s, x_peer)

    def msg_c(l, e, j):
        ref = hids[l].at[span(e), lane(j)]
        return rdma(ref, ref, s_c.at[l, e], r_c.at[l, e], s, c_peer)

    def msg_f(l, e, j):
        ref = hids[l].at[span(e), lane(j)]
        return rdma(ref, ref, s_f.at[l, e], r_f.at[l, e], s, c_peer)

    def msg_h(l, src, dst, d):
        hid = hids[l]
        return rdma(
            hid.at[span(src), lane(w)], hid.at[span(dst), lane(w)],
            s_h.at[l, dst], r_h.at[l, dst], s + d, w,
        )

    def emit(l, c, state):
        value = state.astype(jnp.float32) * scales[l][...][None, :] + shifts[l][...][None, :]
        hidden = jax.nn.gelu(value, approximate=True).astype(jnp.bfloat16)
        e = c + edge[l]
        hids[l][span(e), lane(w)] = hidden
        if edge[l]:
            @pl.when(jnp.logical_and(c < edge[l], has_prev))
            def _():
                msg_h(l, e, nc + e, -1).start()

            @pl.when(jnp.logical_and(c >= nc - edge[l], has_next))
            def _():
                msg_h(l, e, e - nc, 1).start()

        msg_x(l, e, w).start()
        msg_c(l, e, w).start()

    def halos(l):
        out = []
        for c in makes:
            if c >= nc - edge[l]:
                out.append((c - (nc - edge[l]), has_prev))
            if c < edge[l]:
                out.append((nc + edge[l] + c, has_next))
        return out

    def halo_arrive(l, e, there):
        @pl.when(there)
        def _():
            msg_h(l, e, e, 1).wait_recv()
            msg_x(l, e, w).start()
            msg_c(l, e, w).start()

        @pl.when(jnp.logical_not(there))
        def _():
            hids[l][span(e), :] = jnp.zeros((CHUNK, m * cols), jnp.bfloat16)

    def forward(l, e, there=None):
        def go():
            msg_x(l, e, x_peer).wait_recv()
            msg_f(l, e, x_peer).start()

        if there is None:
            go()
        else:
            pl.when(there)(go)

    def ready(l, e, there=None):
        def go():
            msg_c(l, e, c_peer).wait_recv()
            msg_f(l, e, xc_peer).wait_recv()

        if there is None:
            go()
        else:
            pl.when(there)(go)

    def sent(l):
        d = edge[l]

        def one_chunk(e):
            msg_x(l, e, w).wait_send()
            msg_c(l, e, w).wait_send()
            msg_f(l, e, x_peer).wait_send()

        for e, there in halos(l):
            @pl.when(there)
            def _():
                one_chunk(e)
        for e in range(d, nc + d):
            one_chunk(e)
        for e in range(d):
            @pl.when(has_prev)
            def _():
                msg_h(l, d + e, nc + d + e, -1).wait_send()

            @pl.when(has_next)
            def _():
                msg_h(l, nc + e, e, 1).wait_send()

    def product(l, e, tap):
        return jnp.dot(
            hids[l][span(e), :], wb[l, tap], preferred_element_type=jnp.float32
        )

    def joined(state, total):
        return (state.astype(jnp.float32) + total).astype(jnp.bfloat16)

    def msg_g(i):
        return rdma(
            part_out.at[i], part_in.at[i], s_g.at[i], r_g.at[i], s + (1 if i == 0 else -1), w
        )

    makes = [1 + (i + nc - 3) % (nc - 2) for i in range(nc - 2)] + [0, nc - 1]

    barrier = pltpu.get_barrier_semaphore()
    peers = [
        (True, y_peer, w), (True, s, x_peer), (True, s, c_peer),
        (up, s + 2, w), (down, s - 2, w), (has_next, s + 1, w), (has_prev, s - 1, w),
    ]
    expected = 3
    for there, ds, dw in peers:
        def greet(ds=ds, dw=dw):
            pl.semaphore_signal(
                barrier, inc=1, device_id=(ds, dw), device_id_type=pl.DeviceIdType.MESH
            )

        if there is True:
            greet()
        else:
            pl.when(there)(greet)
            expected = expected + there.astype(jnp.int32)
    wb[0, :, krows(z, y), :] = w1_ref[...]
    wb[1, :, krows(z, y), :] = w2_ref[...]
    pl.semaphore_wait(barrier, expected)

    weights_start(0)

    @pl.loop(0, nc)
    def _(i):
        emit(0, i, x_ref[span(i), :])

    weights_pair(0)
    k = 1
    for e in range(nc):
        forward(0, e)
        if e % 3 == 1 and k < lines:
            weights_step(0, k)
            k += 1
    for k in range(k, lines):
        weights_step(0, k)
    weights_start(1)
    weights_finish(0)
    for e in range(nc):
        ready(0, e)

    part_out[0] = product(0, nc - 1, 0).astype(jnp.bfloat16)
    part_out[1] = product(0, 0, TAPS - 1).astype(jnp.bfloat16)
    for i, out, back in ((0, has_next, has_prev), (1, has_prev, has_next)):
        pl.when(out)(msg_g(i).start)

        @pl.when(jnp.logical_not(back))
        def _():
            part_in[i] = jnp.zeros((CHUNK, cols), jnp.bfloat16)

    def make(c, total):
        state = joined(x_ref[span(c), :], total)
        one[span(c), :] = state
        emit(1, c, state)

    @pl.loop(0, nc - 2)
    def _(i):
        c = 1 + lax.rem(i + nc - 3, nc - 2)
        make(c, product(0, c - 1, 0) + product(0, c, 1) + product(0, c + 1, 2))

    for i, c, other, tap, back in ((0, 0, 1, 2, has_prev), (1, nc - 1, nc - 2, 0, has_next)):
        total = product(0, c, 1) + product(0, other, tap)
        pl.when(back)(msg_g(i).wait_recv)
        make(c, total + part_in[i].astype(jnp.float32))

    own = [(c + edge[1], None) for c in makes]
    ends = halos(1)
    arrived = set()
    left = list(range(nc))

    def conv_ready():
        for c in list(left):
            needs = [c + tap * reach[1] for tap in range(TAPS)]
            if arrived.issuperset(needs):
                left.remove(c)
                total = product(1, needs[0], 0) + product(1, needs[1], 1) + product(1, needs[2], 2)
                out_ref[span(c), :] = joined(one[span(c), :], total)

    k = 1
    pending = list(ends)
    for i, (e, _) in enumerate(own):
        forward(1, e)
        if i == 1:
            weights_pair(1)
        if i % 3 == 2 and k < lines:
            weights_step(1, k)
            k += 1
        if i >= 5 and pending:
            halo_arrive(1, *pending.pop(0))
    for e, there in pending:
        halo_arrive(1, e, there)
    for k in range(k, lines):
        weights_step(1, k)
    weights_finish(1)
    for e, _ in own:
        ready(1, e)
        arrived.add(e)
    conv_ready()
    for e, there in ends:
        forward(1, e, there)
        ready(1, e, there)
        arrived.add(e)
        conv_ready()

    for i, out in ((0, has_next), (1, has_prev)):
        pl.when(out)(msg_g(i).wait_send)
    for l in range(2):
        sent(l)
        weights_drain(l)


def shards(n, m, x, s1, b1, w1, s2, b2, w2):
    rows, cols = x.shape
    channels = m * cols
    lines = n // 2
    ext = rows // CHUNK + 2 * (DILATION_SECOND // CHUNK)
    dma = pltpu.SemaphoreType.DMA
    vmem = pl.BlockSpec(memory_space=pltpu.VMEM)
    return pl.pallas_call(
        functools.partial(tower_kernel, n, m),
        out_shape=jax.ShapeDtypeStruct((rows, cols), jnp.bfloat16),
        in_specs=[vmem] * 7,
        out_specs=vmem,
        scratch_shapes=[
            pltpu.VMEM((rows, channels), jnp.bfloat16),
            pltpu.VMEM((rows + 2 * DILATION_SECOND, channels), jnp.bfloat16),
            pltpu.VMEM((2, TAPS, channels, cols), jnp.bfloat16),
            pltpu.VMEM((rows, cols), jnp.bfloat16),
            pltpu.VMEM((2, CHUNK, cols), jnp.bfloat16),
            pltpu.VMEM((2, CHUNK, cols), jnp.bfloat16),
            dma((2,)), dma((2,)),
            dma((2, 2, lines)), dma((2, lines)),
            dma((2, 2, lines)), dma((2, lines)),
            dma((2, lines)), dma((2, lines)),
        ] + [dma((2, ext))] * 8,
        compiler_params=pltpu.CompilerParams(
            collective_id=0, has_side_effects=True, vmem_limit_bytes=56 * 1024 * 1024
        ),
        cost_estimate=pl.CostEstimate(
            flops=4 * TAPS * rows * channels * cols,
            bytes_accessed=4 * rows * cols + 4 * TAPS * w1.shape[1] * cols,
            transcendentals=2 * rows * cols,
        ),
    )(x, s1, b1, w1, s2, b2, w2)


def solution(mesh):
    placed = (
        P("seq", "wt"),
        P("wt"),
        P("wt"),
        P(None, "seq", "wt"),
        P("wt"),
        P("wt"),
        P(None, "seq", "wt"),
    )
    n, m = mesh.shape["seq"], mesh.shape["wt"]
    return jax.shard_map(
        functools.partial(shards, n, m), mesh=mesh, in_specs=placed,
        out_specs=P("seq", "wt"), check_vma=False,
    )
```

```python
import functools

import jax
import jax.numpy as jnp
from jax import lax
from jax.experimental import pallas as pl
from jax.experimental.pallas import tpu as pltpu
from jax.sharding import PartitionSpec as P

DILATION_FIRST = 256
DILATION_SECOND = 512
CHUNK = 256
TAPS = 3
ORDER = (0, 2, 1)
LAST = ORDER[-1]


def tower_kernel(
    n, m, x_ref, s1_ref, b1_ref, w1_ref, s2_ref, b2_ref, w2_ref, out_ref,
    hid1, hid2, wb, one, acc, part_out, part_in, s_g, r_g,
    s_p, r_p, s_q, r_q, s_y, r_y, s_x, r_x, s_c, r_c, s_f, r_f,
):
    s = lax.axis_index("seq")
    w = lax.axis_index("wt")
    lines = n // 2
    z, y = s // 2, lax.rem(s, 2)
    x_peer = lax.rem(w + m // 2, m)
    c_peer = w + 1 - 2 * lax.rem(w, 2)
    xc_peer = lax.rem(c_peer + m // 2, m)
    y_peer = s + 1 - 2 * y
    rows, cols = x_ref.shape
    kr = w1_ref.shape[1]
    nc = rows // CHUNK
    reach = (DILATION_FIRST // CHUNK, DILATION_SECOND // CHUNK)
    hids = (hid1, hid2)
    scales = (s1_ref, s2_ref)
    shifts = (b1_ref, b2_ref)
    has_prev, has_next = s > 0, s < n - 1
    up, down = z < lines - 1, z > 0
    steps = ((1, up), (-1, down))

    def rdma(src, dst, ss, rs, ds, dw):
        return pltpu.make_async_remote_copy(
            src_ref=src, dst_ref=dst, send_sem=ss, recv_sem=rs,
            device_id=(ds, dw), device_id_type=pl.DeviceIdType.MESH,
        )

    def span(e):
        return pl.ds(pl.multiple_of(e * CHUNK, CHUNK), CHUNK)

    def lane(j):
        return pl.ds(pl.multiple_of(j * cols, cols), cols)

    def krows(zz, yy):
        return pl.ds(pl.multiple_of((zz * 2 + yy) * kr, kr), kr)

    def msg_p(l, tap, zz, d):
        ref = wb.at[l, tap, krows(zz, y), :]
        i, j = (0 if d > 0 else 1), l * TAPS + tap
        return rdma(ref, ref, s_p.at[i, j, zz], r_p.at[j, zz], s + 2 * d, w)

    def msg_q(l, zz, d):
        ref = wb.at[l, LAST, krows(zz, 1 - y), :]
        i = 0 if d > 0 else 1
        return rdma(ref, ref, s_q.at[i, l, zz], r_q.at[l, zz], s + 2 * d, w)

    def msg_y(l, tap, zz, yy):
        ref = wb.at[l, tap, krows(zz, yy), :]
        j = l * TAPS + tap
        return rdma(ref, ref, s_y.at[j, zz], r_y.at[j, zz], y_peer, w)

    def weights_start(l, tap):
        if tap == ORDER[1]:
            msg_y(l, LAST, z, y).start()
        if tap == LAST:
            msg_y(l, LAST, z, 1 - y).wait_recv()
        else:
            msg_y(l, tap, z, y).start()
        for d, there in steps:
            @pl.when(there)
            def _():
                msg_p(l, tap, z, d).start()
                if tap == LAST:
                    msg_q(l, z, d).start()

    def weights_step(l, tap, k):
        for d, there in steps:
            zz = z - d * k

            @pl.when(jnp.logical_and(zz >= 0, zz < lines))
            def _():
                msg_p(l, tap, zz, d).wait_recv()
                pl.when(there)(msg_p(l, tap, zz, d).start)
                if tap == LAST:
                    msg_q(l, zz, d).wait_recv()
                    pl.when(there)(msg_q(l, zz, d).start)
                else:
                    msg_y(l, tap, zz, y).start()

    def weights_finish(l, tap):
        if tap == LAST:
            return
        msg_y(l, tap, z, 1 - y).wait_recv()
        for k in range(1, lines):
            for d in (1, -1):
                zz = z - d * k
                pl.when(jnp.logical_and(zz >= 0, zz < lines))(
                    msg_y(l, tap, zz, 1 - y).wait_recv
                )

    def weights_drain(l):
        for tap in range(TAPS):
            msg_y(l, tap, z, y).wait_send()
            for k in range(lines):
                for d, there in steps:
                    zz = z - d * k

                    @pl.when(jnp.logical_and(zz >= 0, zz < lines))
                    def _():
                        if k and tap != LAST:
                            msg_y(l, tap, zz, y).wait_send()

                        @pl.when(there)
                        def _():
                            msg_p(l, tap, zz, d).wait_send()
                            if tap == LAST:
                                msg_q(l, zz, d).wait_send()

    def msg_x(l, e, j):
        ref = hids[l].at[span(e), lane(j)]
        return rdma(ref, ref, s_x.at[l, e], r_x.at[l, e], s, x_peer)

    def msg_c(l, e, j):
        ref = hids[l].at[span(e), lane(j)]
        return rdma(ref, ref, s_c.at[l, e], r_c.at[l, e], s, c_peer)

    def msg_f(l, e, j):
        ref = hids[l].at[span(e), lane(j)]
        return rdma(ref, ref, s_f.at[l, e], r_f.at[l, e], s, c_peer)

    def emit(l, c, state):
        value = state.astype(jnp.float32) * scales[l][...][None, :] + shifts[l][...][None, :]
        hids[l][span(c), lane(w)] = jax.nn.gelu(value, approximate=True).astype(jnp.bfloat16)
        msg_x(l, c, w).start()
        msg_c(l, c, w).start()

    def forward(l, e):
        msg_x(l, e, x_peer).wait_recv()
        msg_f(l, e, x_peer).start()

    def ready(l, e):
        msg_c(l, e, c_peer).wait_recv()
        msg_f(l, e, xc_peer).wait_recv()

    def sent(l):
        for e in range(nc):
            msg_x(l, e, w).wait_send()
            msg_c(l, e, w).wait_send()
            msg_f(l, e, x_peer).wait_send()

    def product(l, e, tap):
        return jnp.dot(
            hids[l][span(e), :], wb[l, tap], preferred_element_type=jnp.float32
        )

    states = (x_ref, one)

    def msg_g(l, i):
        ref = pl.ds(0, reach[l] * CHUNK)
        return rdma(
            part_out.at[l, i, ref, :], part_in.at[l, i, ref, :],
            s_g.at[l, i], r_g.at[l, i], s + (1 if i == 0 else -1), w,
        )

    def tap_first(l, lo, hi):
        d = reach[l]
        cut = nc - d
        if lo == 0:
            head = pl.ds(0, d * CHUNK)
            acc[head, :] = states[l][head, :].astype(jnp.float32)

        if lo < min(hi, cut):
            @pl.loop(lo, min(hi, cut))
            def _(e):
                acc[span(e + d), :] = states[l][span(e + d), :].astype(jnp.float32) + product(l, e, 0)

        if max(lo, cut) < hi:
            @pl.loop(max(lo, cut), hi)
            def _(e):
                part_out[l, 0, span(e - cut), :] = product(l, e, 0).astype(jnp.bfloat16)

        if hi == nc:
            pl.when(has_next)(msg_g(l, 0).start)

    def tap_third(l, lo, hi):
        d = reach[l]
        if lo < d:
            @pl.loop(lo, min(hi, d))
            def _(e):
                part_out[l, 1, span(e), :] = product(l, e, TAPS - 1).astype(jnp.bfloat16)

            if hi >= d:
                pl.when(has_prev)(msg_g(l, 1).start)

        if max(lo, d) < hi:
            @pl.loop(max(lo, d), hi)
            def _(e):
                acc[span(e - d), :] += product(l, e, TAPS - 1)

    def neighbours(l):
        count = reach[l] * CHUNK
        for i, there, at in ((0, has_prev, 0), (1, has_next, rows - count)):
            @pl.when(there)
            def _():
                msg_g(l, i).wait_recv()
                acc[pl.ds(at, count), :] += part_in[l, i, pl.ds(0, count), :].astype(jnp.float32)

    def tap_middle(l, lo, hi):
        @pl.loop(lo, hi)
        def _(c):
            state = (acc[span(c), :] + product(l, c, 1)).astype(jnp.bfloat16)
            if l == 0:
                one[span(c), :] = state
                emit(1, c, state)
            else:
                out_ref[span(c), :] = state

    def events():
        out = []
        slots = [(l, tap) for l in range(2) for tap in ORDER]
        half = nc // 2
        for l, base in ((0, 0.0), (1, 44.0)):
            ends = {}
            for i, tap in enumerate(ORDER):
                length = 21.0 if tap == LAST else 10.5
                at = base + 10.5 * i
                for k in range(1, lines):
                    when = at + length * k / (lines - 1)
                    out.append((when, functools.partial(weights_step, l, tap, k)))
                    follows = slots.index((l, tap)) + 1
                    if k == (max(1, lines - 2) if tap == LAST else 1) and follows < len(slots):
                        out.append((when, functools.partial(weights_start, *slots[follows])))
                ends[tap] = at + length + (0.0 if tap == LAST else 5.0)
            here = [base + 1.0 + 36.8 * (e + 1) / nc for e in range(nc)]
            for e in range(nc):
                out.append((here[e], functools.partial(forward, l, e)))
                out.append((here[e] + 1.5, functools.partial(ready, l, e)))
            out.append((ends[0], functools.partial(weights_finish, l, 0)))
            out.append((ends[2], functools.partial(weights_finish, l, 2)))
            for lo in range(0, nc, 2):
                hi = min(lo + 2, nc)
                first = max(here[hi - 1] + 1.6, ends[0] + 0.1)
                third = max(here[hi - 1] + 1.7, ends[2] + 0.1)
                out.append((first, functools.partial(tap_first, l, lo, hi)))
                out.append((third, functools.partial(tap_third, l, lo, hi)))
            done = max(ends[LAST], here[-1] + 2.0) + 0.1
            out.append((done, functools.partial(neighbours, l)))
            out.append((done, functools.partial(tap_middle, l, 0, half)))
            out.append((done + 4.0, functools.partial(tap_middle, l, half, nc)))
        return [go for _, go in sorted(out, key=lambda entry: entry[0])]

    barrier = pltpu.get_barrier_semaphore()
    peers = [
        (True, y_peer, w), (True, s, x_peer), (True, s, c_peer),
        (up, s + 2, w), (down, s - 2, w), (has_next, s + 1, w), (has_prev, s - 1, w),
    ]
    expected = 3
    for there, ds, dw in peers:
        def greet(ds=ds, dw=dw):
            pl.semaphore_signal(
                barrier, inc=1, device_id=(ds, dw), device_id_type=pl.DeviceIdType.MESH
            )

        if there is True:
            greet()
        else:
            pl.when(there)(greet)
            expected = expected + there.astype(jnp.int32)
    wb[0, :, krows(z, y), :] = w1_ref[...]
    wb[1, :, krows(z, y), :] = w2_ref[...]
    pl.semaphore_wait(barrier, expected)

    weights_start(0, ORDER[0])

    @pl.loop(0, nc)
    def _(i):
        emit(0, i, x_ref[span(i), :])

    for go in events():
        go()

    for l in range(2):
        sent(l)
        weights_drain(l)
        pl.when(has_next)(msg_g(l, 0).wait_send)
        pl.when(has_prev)(msg_g(l, 1).wait_send)


def shards(n, m, x, s1, b1, w1, s2, b2, w2):
    rows, cols = x.shape
    channels = m * cols
    lines = n // 2
    dma = pltpu.SemaphoreType.DMA
    vmem = pl.BlockSpec(memory_space=pltpu.VMEM)
    return pl.pallas_call(
        functools.partial(tower_kernel, n, m),
        out_shape=jax.ShapeDtypeStruct((rows, cols), jnp.bfloat16),
        in_specs=[vmem] * 7,
        out_specs=vmem,
        scratch_shapes=[
            pltpu.VMEM((rows, channels), jnp.bfloat16),
            pltpu.VMEM((rows, channels), jnp.bfloat16),
            pltpu.VMEM((2, TAPS, channels, cols), jnp.bfloat16),
            pltpu.VMEM((rows, cols), jnp.bfloat16),
            pltpu.VMEM((rows, cols), jnp.float32),
            pltpu.VMEM((2, 2, DILATION_SECOND, cols), jnp.bfloat16),
            pltpu.VMEM((2, 2, DILATION_SECOND, cols), jnp.bfloat16),
            dma((2, 2)), dma((2, 2)),
            dma((2, 2 * TAPS, lines)), dma((2 * TAPS, lines)),
            dma((2, 2, lines)), dma((2, lines)),
            dma((2 * TAPS, lines)), dma((2 * TAPS, lines)),
        ] + [dma((2, rows // CHUNK))] * 6,
        compiler_params=pltpu.CompilerParams(
            collective_id=0, has_side_effects=True, vmem_limit_bytes=56 * 1024 * 1024
        ),
        cost_estimate=pl.CostEstimate(
            flops=4 * TAPS * rows * channels * cols,
            bytes_accessed=4 * rows * cols + 4 * TAPS * w1.shape[1] * cols,
            transcendentals=2 * rows * cols,
        ),
    )(x, s1, b1, w1, s2, b2, w2)


def solution(mesh):
    placed = (
        P("seq", "wt"),
        P("wt"),
        P("wt"),
        P(None, "seq", "wt"),
        P("wt"),
        P("wt"),
        P(None, "seq", "wt"),
    )
    n, m = mesh.shape["seq"], mesh.shape["wt"]
    return jax.shard_map(
        functools.partial(shards, n, m), mesh=mesh, in_specs=placed,
        out_specs=P("seq", "wt"), check_vma=False,
    )
```

```python
import functools

import jax
import jax.numpy as jnp
from jax import lax
from jax.experimental import pallas as pl
from jax.experimental.pallas import tpu as pltpu
from jax.sharding import PartitionSpec as P

DILATION_FIRST = 256
DILATION_SECOND = 512
CHUNK = 256
TAPS = 3
ORDER = (0, 2, 1)
LAST = ORDER[-1]


def tower_kernel(
    n, m, x_ref, s1_ref, b1_ref, w1_ref, s2_ref, b2_ref, w2_ref, out_ref,
    hid1, hid2, wb, one, acc, part_out, part_in, s_g, r_g,
    s_p, r_p, s_y, r_y, s_x, r_x, s_c, r_c, s_f, r_f,
):
    s = lax.axis_index("seq")
    w = lax.axis_index("wt")
    lines = n // 2
    z, y = s // 2, lax.rem(s, 2)
    x_peer = lax.rem(w + m // 2, m)
    c_peer = w + 1 - 2 * lax.rem(w, 2)
    xc_peer = lax.rem(c_peer + m // 2, m)
    y_peer = s + 1 - 2 * y
    rows, cols = x_ref.shape
    kr = w1_ref.shape[1]
    nc = rows // CHUNK
    reach = (DILATION_FIRST // CHUNK, DILATION_SECOND // CHUNK)
    hids = (hid1, hid2)
    scales = (s1_ref, s2_ref)
    shifts = (b1_ref, b2_ref)
    has_prev, has_next = s > 0, s < n - 1

    def rdma(src, dst, ss, rs, ds, dw):
        return pltpu.make_async_remote_copy(
            src_ref=src, dst_ref=dst, send_sem=ss, recv_sem=rs,
            device_id=(ds, dw), device_id_type=pl.DeviceIdType.MESH,
        )

    def span(e):
        return pl.ds(pl.multiple_of(e * CHUNK, CHUNK), CHUNK)

    def lane(j):
        return pl.ds(pl.multiple_of(j * cols, cols), cols)

    def krows(zz, yy):
        return pl.ds(pl.multiple_of((zz * 2 + yy) * kr, kr), kr)

    def others(go):
        for k in range(1, lines):
            for d in (1, -1):
                zz = z + d * k
                pl.when(jnp.logical_and(zz >= 0, zz < lines))(functools.partial(go, zz))

    def msg_p(l, tap, src, dst):
        ref = wb.at[l, tap, krows(src, y), :]
        j = l * TAPS + tap
        return rdma(ref, ref, s_p.at[j, dst], r_p.at[j, src], dst * 2 + y, w)

    def msg_y(l, tap, zz, yy):
        ref = wb.at[l, tap, krows(zz, yy), :]
        j = l * TAPS + tap
        return rdma(ref, ref, s_y.at[j, zz], r_y.at[j, zz], y_peer, w)

    def weights_start(l, tap):
        msg_y(l, tap, z, y).start()
        others(lambda zz: msg_p(l, tap, z, zz).start())

    def weights_step(l, tap, k):
        for d in (1, -1):
            zz = z - d * k

            @pl.when(jnp.logical_and(zz >= 0, zz < lines))
            def _():
                msg_p(l, tap, zz, z).wait_recv()
                msg_y(l, tap, zz, y).start()

    def weights_finish(l, tap):
        msg_y(l, tap, z, 1 - y).wait_recv()
        others(lambda zz: msg_y(l, tap, zz, 1 - y).wait_recv())

    def weights_drain(l):
        for tap in range(TAPS):
            msg_y(l, tap, z, y).wait_send()
            others(lambda zz: msg_y(l, tap, zz, y).wait_send())
            others(lambda zz: msg_p(l, tap, z, zz).wait_send())

    def msg_x(l, e, j):
        ref = hids[l].at[span(e), lane(j)]
        return rdma(ref, ref, s_x.at[l, e], r_x.at[l, e], s, x_peer)

    def msg_c(l, e, j):
        ref = hids[l].at[span(e), lane(j)]
        return rdma(ref, ref, s_c.at[l, e], r_c.at[l, e], s, c_peer)

    def msg_f(l, e, j):
        ref = hids[l].at[span(e), lane(j)]
        return rdma(ref, ref, s_f.at[l, e], r_f.at[l, e], s, c_peer)

    def emit(l, c, state):
        value = state.astype(jnp.float32) * scales[l][...][None, :] + shifts[l][...][None, :]
        hids[l][span(c), lane(w)] = jax.nn.gelu(value, approximate=True).astype(jnp.bfloat16)
        msg_x(l, c, w).start()
        msg_c(l, c, w).start()

    def forward(l, e):
        msg_x(l, e, x_peer).wait_recv()
        msg_f(l, e, x_peer).start()

    def ready(l, e):
        msg_c(l, e, c_peer).wait_recv()
        msg_f(l, e, xc_peer).wait_recv()

    def sent(l):
        for e in range(nc):
            msg_x(l, e, w).wait_send()
            msg_c(l, e, w).wait_send()
            msg_f(l, e, x_peer).wait_send()

    def product(l, e, tap):
        return jnp.dot(
            hids[l][span(e), :], wb[l, tap], preferred_element_type=jnp.float32
        )

    states = (x_ref, one)

    def msg_g(l, i):
        ref = pl.ds(0, reach[l] * CHUNK)
        return rdma(
            part_out.at[l, i, ref, :], part_in.at[l, i, ref, :],
            s_g.at[l, i], r_g.at[l, i], s + (1 if i == 0 else -1), w,
        )

    def tap_first(l, lo, hi):
        d = reach[l]
        cut = nc - d
        if lo == 0:
            head = pl.ds(0, d * CHUNK)
            acc[head, :] = states[l][head, :].astype(jnp.float32)

        if lo < min(hi, cut):
            @pl.loop(lo, min(hi, cut))
            def _(e):
                acc[span(e + d), :] = states[l][span(e + d), :].astype(jnp.float32) + product(l, e, 0)

        if max(lo, cut) < hi:
            @pl.loop(max(lo, cut), hi)
            def _(e):
                part_out[l, 0, span(e - cut), :] = product(l, e, 0).astype(jnp.bfloat16)

        if hi == nc:
            pl.when(has_next)(msg_g(l, 0).start)

    def tap_third(l, lo, hi):
        d = reach[l]
        if lo < d:
            @pl.loop(lo, min(hi, d))
            def _(e):
                part_out[l, 1, span(e), :] = product(l, e, TAPS - 1).astype(jnp.bfloat16)

            if hi >= d:
                pl.when(has_prev)(msg_g(l, 1).start)

        if max(lo, d) < hi:
            @pl.loop(max(lo, d), hi)
            def _(e):
                acc[span(e - d), :] += product(l, e, TAPS - 1)

    def neighbours(l):
        count = reach[l] * CHUNK
        for i, there, at in ((0, has_prev, 0), (1, has_next, rows - count)):
            @pl.when(there)
            def _():
                msg_g(l, i).wait_recv()
                acc[pl.ds(at, count), :] += part_in[l, i, pl.ds(0, count), :].astype(jnp.float32)

    def tap_middle(l, lo, hi):
        @pl.loop(lo, hi)
        def _(c):
            state = (acc[span(c), :] + product(l, c, 1)).astype(jnp.bfloat16)
            if l == 0:
                one[span(c), :] = state
                emit(1, c, state)
            else:
                out_ref[span(c), :] = state

    def events():
        out = []
        slots = [(l, tap) for l in range(2) for tap in ORDER]
        half = nc // 2
        for l, base in ((0, 0.0), (1, 44.0)):
            ends = {}
            for i, tap in enumerate(ORDER):
                at = base + 14.0 * i
                for k in range(1, lines):
                    when = at + 10.5 * k / (lines - 1)
                    out.append((when, functools.partial(weights_step, l, tap, k)))
                    follows = slots.index((l, tap)) + 1
                    if k == 1 and follows < len(slots):
                        out.append((when, functools.partial(weights_start, *slots[follows])))
                ends[tap] = at + 14.5
                out.append((ends[tap], functools.partial(weights_finish, l, tap)))
            here = [base + 1.0 + 36.8 * (e + 1) / nc for e in range(nc)]
            for e in range(nc):
                out.append((here[e], functools.partial(forward, l, e)))
                out.append((here[e] + 1.5, functools.partial(ready, l, e)))
            for lo in range(0, nc, 2):
                hi = min(lo + 2, nc)
                first = max(here[hi - 1] + 1.6, ends[0] + 0.1)
                third = max(here[hi - 1] + 1.7, ends[2] + 0.1)
                out.append((first, functools.partial(tap_first, l, lo, hi)))
                out.append((third, functools.partial(tap_third, l, lo, hi)))
            done = max(ends[LAST], here[-1] + 2.0) + 0.1
            out.append((done, functools.partial(neighbours, l)))
            out.append((done, functools.partial(tap_middle, l, 0, half)))
            out.append((done + 4.0, functools.partial(tap_middle, l, half, nc)))
        return [go for _, go in sorted(out, key=lambda entry: entry[0])]

    barrier = pltpu.get_barrier_semaphore()
    peers = [
        (True, y_peer, w), (True, s, x_peer), (True, s, c_peer),
        (has_next, s + 1, w), (has_prev, s - 1, w),
    ]
    for k in range(1, lines):
        peers += [(z + k < lines, s + 2 * k, w), (z - k >= 0, s - 2 * k, w)]
    expected = 3
    for there, ds, dw in peers:
        def greet(ds=ds, dw=dw):
            pl.semaphore_signal(
                barrier, inc=1, device_id=(ds, dw), device_id_type=pl.DeviceIdType.MESH
            )

        if there is True:
            greet()
        else:
            pl.when(there)(greet)
            expected = expected + there.astype(jnp.int32)
    wb[0, :, krows(z, y), :] = w1_ref[...]
    wb[1, :, krows(z, y), :] = w2_ref[...]
    pl.semaphore_wait(barrier, expected)

    weights_start(0, ORDER[0])

    @pl.loop(0, nc)
    def _(i):
        emit(0, i, x_ref[span(i), :])

    for go in events():
        go()

    for l in range(2):
        sent(l)
        weights_drain(l)
        pl.when(has_next)(msg_g(l, 0).wait_send)
        pl.when(has_prev)(msg_g(l, 1).wait_send)


def shards(n, m, x, s1, b1, w1, s2, b2, w2):
    rows, cols = x.shape
    channels = m * cols
    lines = n // 2
    dma = pltpu.SemaphoreType.DMA
    vmem = pl.BlockSpec(memory_space=pltpu.VMEM)
    return pl.pallas_call(
        functools.partial(tower_kernel, n, m),
        out_shape=jax.ShapeDtypeStruct((rows, cols), jnp.bfloat16),
        in_specs=[vmem] * 7,
        out_specs=vmem,
        scratch_shapes=[
            pltpu.VMEM((rows, channels), jnp.bfloat16),
            pltpu.VMEM((rows, channels), jnp.bfloat16),
            pltpu.VMEM((2, TAPS, channels, cols), jnp.bfloat16),
            pltpu.VMEM((rows, cols), jnp.bfloat16),
            pltpu.VMEM((rows, cols), jnp.float32),
            pltpu.VMEM((2, 2, DILATION_SECOND, cols), jnp.bfloat16),
            pltpu.VMEM((2, 2, DILATION_SECOND, cols), jnp.bfloat16),
            dma((2, 2)), dma((2, 2)),
            dma((2 * TAPS, lines)), dma((2 * TAPS, lines)),
            dma((2 * TAPS, lines)), dma((2 * TAPS, lines)),
        ] + [dma((2, rows // CHUNK))] * 6,
        compiler_params=pltpu.CompilerParams(
            collective_id=0, has_side_effects=True, vmem_limit_bytes=56 * 1024 * 1024
        ),
        cost_estimate=pl.CostEstimate(
            flops=4 * TAPS * rows * channels * cols,
            bytes_accessed=4 * rows * cols + 4 * TAPS * w1.shape[1] * cols,
            transcendentals=2 * rows * cols,
        ),
    )(x, s1, b1, w1, s2, b2, w2)


def solution(mesh):
    placed = (
        P("seq", "wt"),
        P("wt"),
        P("wt"),
        P(None, "seq", "wt"),
        P("wt"),
        P("wt"),
        P(None, "seq", "wt"),
    )
    n, m = mesh.shape["seq"], mesh.shape["wt"]
    return jax.shard_map(
        functools.partial(shards, n, m), mesh=mesh, in_specs=placed,
        out_specs=P("seq", "wt"), check_vma=False,
    )
```

```python
import functools

import jax
import jax.numpy as jnp
from jax import lax
from jax.experimental import pallas as pl
from jax.experimental.pallas import tpu as pltpu
from jax.sharding import PartitionSpec as P

DILATION_FIRST = 256
DILATION_SECOND = 512
CHUNK = 256
TAPS = 3
ORDER = (0, 2, 1)
LAST = ORDER[-1]


def tower_kernel(
    n, m, x_ref, s1_ref, b1_ref, w1_ref, s2_ref, b2_ref, w2_ref, out_ref,
    hid1, hid2, wb, acc, part_out, part_in, s_g, r_g,
    s_p, r_p, s_q, r_q, s_y, r_y, s_x, r_x, s_c, r_c, s_f, r_f,
):
    s = lax.axis_index("seq")
    w = lax.axis_index("wt")
    lines = n // 2
    z, y = s // 2, lax.rem(s, 2)
    x_peer = lax.rem(w + m // 2, m)
    c_peer = w + 1 - 2 * lax.rem(w, 2)
    xc_peer = lax.rem(c_peer + m // 2, m)
    y_peer = s + 1 - 2 * y
    rows, cols = x_ref.shape
    kr = w1_ref.shape[1]
    nc = rows // CHUNK
    reach = (DILATION_FIRST // CHUNK, DILATION_SECOND // CHUNK)
    hids = (hid1, hid2)
    scales = (s1_ref, s2_ref)
    shifts = (b1_ref, b2_ref)
    has_prev, has_next = s > 0, s < n - 1
    up, down = z < lines - 1, z > 0
    steps = ((1, up), (-1, down))

    def rdma(src, dst, ss, rs, ds, dw):
        return pltpu.make_async_remote_copy(
            src_ref=src, dst_ref=dst, send_sem=ss, recv_sem=rs,
            device_id=(ds, dw), device_id_type=pl.DeviceIdType.MESH,
        )

    def span(e):
        return pl.ds(pl.multiple_of(e * CHUNK, CHUNK), CHUNK)

    def lane(j):
        return pl.ds(pl.multiple_of(j * cols, cols), cols)

    def krows(zz, yy):
        return pl.ds(pl.multiple_of((zz * 2 + yy) * kr, kr), kr)

    def msg_p(l, tap, zz, d):
        ref = wb.at[l, tap, krows(zz, y), :]
        i, j = (0 if d > 0 else 1), l * TAPS + tap
        return rdma(ref, ref, s_p.at[i, j, zz], r_p.at[j, zz], s + 2 * d, w)

    def msg_q(l, zz, d):
        ref = wb.at[l, LAST, krows(zz, 1 - y), :]
        i = 0 if d > 0 else 1
        return rdma(ref, ref, s_q.at[i, l, zz], r_q.at[l, zz], s + 2 * d, w)

    def msg_y(l, tap, zz, yy):
        ref = wb.at[l, tap, krows(zz, yy), :]
        j = l * TAPS + tap
        return rdma(ref, ref, s_y.at[j, zz], r_y.at[j, zz], y_peer, w)

    def weights_start(l, tap):
        if tap == ORDER[1]:
            msg_y(l, LAST, z, y).start()
        if tap == LAST:
            msg_y(l, LAST, z, 1 - y).wait_recv()
        else:
            msg_y(l, tap, z, y).start()
        for d, there in steps:
            @pl.when(there)
            def _():
                msg_p(l, tap, z, d).start()
                if tap == LAST:
                    msg_q(l, z, d).start()

    def weights_step(l, tap, k):
        low = z < lines // 2
        pl.when(low)(lambda: relay(l, tap, k, steps[::-1]))
        pl.when(jnp.logical_not(low))(lambda: relay(l, tap, k, steps))

    def relay(l, tap, k, ways):
        for d, there in ways:
            zz = z - d * k

            @pl.when(jnp.logical_and(zz >= 0, zz < lines))
            def _():
                msg_p(l, tap, zz, d).wait_recv()
                pl.when(there)(msg_p(l, tap, zz, d).start)
                if tap == LAST:
                    msg_q(l, zz, d).wait_recv()
                    pl.when(there)(msg_q(l, zz, d).start)
                else:
                    msg_y(l, tap, zz, y).start()

    def weights_finish(l, tap):
        if tap == LAST:
            return
        msg_y(l, tap, z, 1 - y).wait_recv()
        for k in range(1, lines):
            for d in (1, -1):
                zz = z - d * k
                pl.when(jnp.logical_and(zz >= 0, zz < lines))(
                    msg_y(l, tap, zz, 1 - y).wait_recv
                )

    def weights_drain(l):
        for tap in range(TAPS):
            msg_y(l, tap, z, y).wait_send()
            for k in range(lines):
                for d, there in steps:
                    zz = z - d * k

                    @pl.when(jnp.logical_and(zz >= 0, zz < lines))
                    def _():
                        if k and tap != LAST:
                            msg_y(l, tap, zz, y).wait_send()

                        @pl.when(there)
                        def _():
                            msg_p(l, tap, zz, d).wait_send()
                            if tap == LAST:
                                msg_q(l, zz, d).wait_send()

    def msg_x(l, e, j):
        ref = hids[l].at[span(e), lane(j)]
        return rdma(ref, ref, s_x.at[l, e], r_x.at[l, e], s, x_peer)

    def msg_c(l, e, j):
        ref = hids[l].at[span(e), lane(j)]
        return rdma(ref, ref, s_c.at[l, e], r_c.at[l, e], s, c_peer)

    def msg_f(l, e, j):
        ref = hids[l].at[span(e), lane(j)]
        return rdma(ref, ref, s_f.at[l, e], r_f.at[l, e], s, c_peer)

    def emit(l, c, state):
        value = state.astype(jnp.float32) * scales[l][...][None, :] + shifts[l][...][None, :]
        hids[l][span(c), lane(w)] = jax.nn.gelu(value, approximate=True).astype(jnp.bfloat16)
        msg_x(l, c, w).start()
        msg_c(l, c, w).start()

    def forward(l, e):
        msg_x(l, e, x_peer).wait_recv()
        msg_f(l, e, x_peer).start()

    def ready(l, e):
        msg_c(l, e, c_peer).wait_recv()
        msg_f(l, e, xc_peer).wait_recv()

    def sent(l):
        for e in range(nc):
            msg_x(l, e, w).wait_send()
            msg_c(l, e, w).wait_send()
            msg_f(l, e, x_peer).wait_send()

    def product(l, e, tap):
        return jnp.dot(
            hids[l][span(e), :], wb[l, tap], preferred_element_type=jnp.float32
        )

    def msg_g(l, i):
        ref = pl.ds(0, reach[l] * CHUNK)
        return rdma(
            part_out.at[l, i, ref, :], part_in.at[l, i, ref, :],
            s_g.at[l, i], r_g.at[l, i], s + (1 if i == 0 else -1), w,
        )

    def tap_first(l, lo, hi):
        d = reach[l]
        cut = nc - d
        if lo < min(hi, cut):
            @pl.loop(lo, min(hi, cut))
            def _(e):
                acc[span(e + d), :] += product(l, e, 0)

        if max(lo, cut) < hi:
            @pl.loop(max(lo, cut), hi)
            def _(e):
                part_out[l, 0, span(e - cut), :] = product(l, e, 0).astype(jnp.bfloat16)

        if hi == nc:
            pl.when(has_next)(msg_g(l, 0).start)

    def tap_third(l, lo, hi):
        d = reach[l]
        if lo < d:
            @pl.loop(lo, min(hi, d))
            def _(e):
                part_out[l, 1, span(e), :] = product(l, e, TAPS - 1).astype(jnp.bfloat16)

            if hi >= d:
                pl.when(has_prev)(msg_g(l, 1).start)

        if max(lo, d) < hi:
            @pl.loop(max(lo, d), hi)
            def _(e):
                acc[span(e - d), :] += product(l, e, TAPS - 1)

    def neighbours(l):
        count = reach[l] * CHUNK
        for i, there, at in ((0, has_prev, 0), (1, has_next, rows - count)):
            @pl.when(there)
            def _():
                msg_g(l, i).wait_recv()
                acc[pl.ds(at, count), :] += part_in[l, i, pl.ds(0, count), :].astype(jnp.float32)

    def tap_middle(l, lo, hi):
        @pl.loop(lo, hi)
        def _(c):
            state = (acc[span(c), :] + product(l, c, 1)).astype(jnp.bfloat16)
            if l == 0:
                acc[span(c), :] = state.astype(jnp.float32)
                emit(1, c, state)
            else:
                out_ref[span(c), :] = state

    last = reach[1]
    groups = [(nc - last, nc)] + [(lo, min(lo + 2, nc - last)) for lo in range(0, nc - last, 2)]
    place = {c: (c + last) % nc for c in range(nc)}

    def events():
        out = []

        def put(when, go, *operands):
            out.append((when, functools.partial(go, *operands)))

        for l, base in ((0, 0.0), (1, 44.0)):
            ends = {}
            for i, tap in enumerate(ORDER):
                length = 21.0 if tap == LAST else 10.5
                at = base + 10.5 * i
                for k in range(1, lines):
                    when = at + length * k / (lines - 1)
                    put(when, weights_step, l, tap, k)
                    if k == max(1, lines - 2):
                        if i == 0:
                            put(when, weights_start, l, LAST)
                        if tap == LAST and l == 0:
                            put(when, weights_start, 1, ORDER[0])
                            put(when, weights_start, 1, ORDER[1])
                ends[tap] = at + length + (0.0 if tap == LAST else 6.0)
            here = [base + 1.0 + 36.8 * (i + 1) / nc for i in range(nc)]
            for i in range(nc):
                e = (i + nc - last) % nc
                put(here[i], forward, l, e)
                put(here[i] + 1.5, ready, l, e)
            put(ends[0], weights_finish, l, 0)
            put(ends[2], weights_finish, l, 2)
            for lo, hi in groups:
                come = here[place[hi - 1]]
                put(max(come + 1.6, ends[0] + 0.1), tap_first, l, lo, hi)
                put(max(come + 1.7, ends[2] + 0.1), tap_third, l, lo, hi)
            done = max(ends[LAST], here[-1] + 2.0) + 0.1
            put(done, neighbours, l)
            for i, (lo, hi) in enumerate(groups):
                put(done + 4.0 * i / len(groups), tap_middle, l, lo, hi)
        return [go for _, go in sorted(out, key=lambda entry: entry[0])]

    barrier = pltpu.get_barrier_semaphore()
    peers = [
        (True, y_peer, w), (True, s, x_peer), (True, s, c_peer),
        (up, s + 2, w), (down, s - 2, w), (has_next, s + 1, w), (has_prev, s - 1, w),
    ]
    expected = 3
    for there, ds, dw in peers:
        def greet(ds=ds, dw=dw):
            pl.semaphore_signal(
                barrier, inc=1, device_id=(ds, dw), device_id_type=pl.DeviceIdType.MESH
            )

        if there is True:
            greet()
        else:
            pl.when(there)(greet)
            expected = expected + there.astype(jnp.int32)
    wb[0, :, krows(z, y), :] = w1_ref[...]
    wb[1, :, krows(z, y), :] = w2_ref[...]
    pl.semaphore_wait(barrier, expected)

    weights_start(0, ORDER[0])
    weights_start(0, ORDER[1])

    @pl.loop(0, nc)
    def _(i):
        c = lax.rem(i + nc - last, nc)
        state = x_ref[span(c), :]
        acc[span(c), :] = state.astype(jnp.float32)
        emit(0, c, state)

    for go in events():
        go()

    for l in range(2):
        sent(l)
        weights_drain(l)
        pl.when(has_next)(msg_g(l, 0).wait_send)
        pl.when(has_prev)(msg_g(l, 1).wait_send)


def shards(n, m, x, s1, b1, w1, s2, b2, w2):
    rows, cols = x.shape
    channels = m * cols
    lines = n // 2
    dma = pltpu.SemaphoreType.DMA
    vmem = pl.BlockSpec(memory_space=pltpu.VMEM)
    return pl.pallas_call(
        functools.partial(tower_kernel, n, m),
        out_shape=jax.ShapeDtypeStruct((rows, cols), jnp.bfloat16),
        in_specs=[vmem] * 7,
        out_specs=vmem,
        scratch_shapes=[
            pltpu.VMEM((rows, channels), jnp.bfloat16),
            pltpu.VMEM((rows, channels), jnp.bfloat16),
            pltpu.VMEM((2, TAPS, channels, cols), jnp.bfloat16),
            pltpu.VMEM((rows, cols), jnp.float32),
            pltpu.VMEM((2, 2, DILATION_SECOND, cols), jnp.bfloat16),
            pltpu.VMEM((2, 2, DILATION_SECOND, cols), jnp.bfloat16),
            dma((2, 2)), dma((2, 2)),
            dma((2, 2 * TAPS, lines)), dma((2 * TAPS, lines)),
            dma((2, 2, lines)), dma((2, lines)),
            dma((2 * TAPS, lines)), dma((2 * TAPS, lines)),
        ] + [dma((2, rows // CHUNK))] * 6,
        compiler_params=pltpu.CompilerParams(
            collective_id=0, has_side_effects=True, vmem_limit_bytes=56 * 1024 * 1024
        ),
        cost_estimate=pl.CostEstimate(
            flops=4 * TAPS * rows * channels * cols,
            bytes_accessed=4 * rows * cols + 4 * TAPS * w1.shape[1] * cols,
            transcendentals=2 * rows * cols,
        ),
    )(x, s1, b1, w1, s2, b2, w2)


def solution(mesh):
    placed = (
        P("seq", "wt"),
        P("wt"),
        P("wt"),
        P(None, "seq", "wt"),
        P("wt"),
        P("wt"),
        P(None, "seq", "wt"),
    )
    n, m = mesh.shape["seq"], mesh.shape["wt"]
    return jax.shard_map(
        functools.partial(shards, n, m), mesh=mesh, in_specs=placed,
        out_specs=P("seq", "wt"), check_vma=False,
    )
```

```python
import functools

import jax
import jax.numpy as jnp
from jax import lax
from jax.experimental import pallas as pl
from jax.experimental.pallas import tpu as pltpu
from jax.sharding import PartitionSpec as P

DILATION_FIRST = 256
DILATION_SECOND = 512
CHUNK = 256
TAPS = 3
ORDER = (0, 2, 1)
LAST = ORDER[-1]


def tower_kernel(
    n, m, x_ref, s1_ref, b1_ref, w1_ref, s2_ref, b2_ref, w2_ref, out_ref,
    hid1, hid2, wb, acc, part_out, part_in, s_g, r_g,
    s_p, r_p, s_q, r_q, s_y, r_y, s_x, r_x, s_c, r_c, s_f, r_f,
):
    s = lax.axis_index("seq")
    w = lax.axis_index("wt")
    lines = n // 2
    z, y = s // 2, lax.rem(s, 2)
    x_peer = lax.rem(w + m // 2, m)
    c_peer = w + 1 - 2 * lax.rem(w, 2)
    xc_peer = lax.rem(c_peer + m // 2, m)
    y_peer = s + 1 - 2 * y
    rows, cols = x_ref.shape
    kr = w1_ref.shape[1]
    nc = rows // CHUNK
    reach = (DILATION_FIRST // CHUNK, DILATION_SECOND // CHUNK)
    hids = (hid1, hid2)
    scales = (s1_ref, s2_ref)
    shifts = (b1_ref, b2_ref)
    has_prev, has_next = s > 0, s < n - 1
    up, down = z < lines - 1, z > 0
    steps = ((1, up), (-1, down))

    def rdma(src, dst, ss, rs, ds, dw):
        return pltpu.make_async_remote_copy(
            src_ref=src, dst_ref=dst, send_sem=ss, recv_sem=rs,
            device_id=(ds, dw), device_id_type=pl.DeviceIdType.MESH,
        )

    def span(e):
        return pl.ds(pl.multiple_of(e * CHUNK, CHUNK), CHUNK)

    def lane(j):
        return pl.ds(pl.multiple_of(j * cols, cols), cols)

    def krows(zz, yy, lo=0, hi=None):
        hi = kr if hi is None else hi
        return pl.ds(pl.multiple_of((zz * 2 + yy) * kr + lo, 16), hi - lo)

    share = (kr // 32 * 16, 0)

    def msg_p(l, tap, zz, d):
        ref = wb.at[l, tap, krows(zz, y), :]
        i, j = (0 if d > 0 else 1), l * TAPS + tap
        return rdma(ref, ref, s_p.at[i, j, zz], r_p.at[j, zz], s + 2 * d, w)

    def msg_q(l, zz, d):
        ref = wb.at[l, LAST, krows(zz, 1 - y, share[l], kr), :]
        i = 0 if d > 0 else 1
        return rdma(ref, ref, s_q.at[i, l, zz], r_q.at[l, zz], s + 2 * d, w)

    def msg_y(l, tap, zz, yy, whole=False):
        part = share[l] if tap == LAST and not whole else kr
        ref = wb.at[l, tap, krows(zz, yy, 0, part), :]
        j = l * TAPS + tap
        return rdma(ref, ref, s_y.at[j, zz], r_y.at[j, zz], y_peer, w)

    def weights_start(l, tap):
        if tap == ORDER[1]:
            msg_y(l, LAST, z, y, True).start()
        if tap == LAST:
            msg_y(l, LAST, z, 1 - y, True).wait_recv()
        else:
            msg_y(l, tap, z, y).start()
        for d, there in steps:
            @pl.when(there)
            def _():
                msg_p(l, tap, z, d).start()
                if tap == LAST:
                    msg_q(l, z, d).start()

    def weights_step(l, tap, k):
        low = z < lines // 2
        pl.when(low)(lambda: relay(l, tap, k, steps[::-1]))
        pl.when(jnp.logical_not(low))(lambda: relay(l, tap, k, steps))

    def relay(l, tap, k, ways):
        for d, there in ways:
            zz = z - d * k

            @pl.when(jnp.logical_and(zz >= 0, zz < lines))
            def _():
                msg_p(l, tap, zz, d).wait_recv()
                pl.when(there)(msg_p(l, tap, zz, d).start)
                if tap == LAST:
                    msg_q(l, zz, d).wait_recv()
                    pl.when(there)(msg_q(l, zz, d).start)
                if tap != LAST or share[l]:
                    msg_y(l, tap, zz, y).start()

    def weights_finish(l, tap):
        if tap == LAST and not share[l]:
            return
        if tap != LAST:
            msg_y(l, tap, z, 1 - y).wait_recv()
        for k in range(1, lines):
            for d in (1, -1):
                zz = z - d * k
                pl.when(jnp.logical_and(zz >= 0, zz < lines))(
                    msg_y(l, tap, zz, 1 - y).wait_recv
                )

    def weights_drain(l):
        for tap in range(TAPS):
            msg_y(l, tap, z, y, True).wait_send()
            for k in range(lines):
                for d, there in steps:
                    zz = z - d * k

                    @pl.when(jnp.logical_and(zz >= 0, zz < lines))
                    def _():
                        if k and (tap != LAST or share[l]):
                            msg_y(l, tap, zz, y).wait_send()

                        @pl.when(there)
                        def _():
                            msg_p(l, tap, zz, d).wait_send()
                            if tap == LAST:
                                msg_q(l, zz, d).wait_send()

    def msg_x(l, e, j):
        ref = hids[l].at[span(e), lane(j)]
        return rdma(ref, ref, s_x.at[l, e], r_x.at[l, e], s, x_peer)

    def msg_c(l, e, j):
        ref = hids[l].at[span(e), lane(j)]
        return rdma(ref, ref, s_c.at[l, e], r_c.at[l, e], s, c_peer)

    def msg_f(l, e, j):
        ref = hids[l].at[span(e), lane(j)]
        return rdma(ref, ref, s_f.at[l, e], r_f.at[l, e], s, c_peer)

    def emit(l, c, state):
        value = state.astype(jnp.float32) * scales[l][...][None, :] + shifts[l][...][None, :]
        hids[l][span(c), lane(w)] = jax.nn.gelu(value, approximate=True).astype(jnp.bfloat16)
        msg_x(l, c, w).start()
        msg_c(l, c, w).start()

    def forward(l, e):
        msg_x(l, e, x_peer).wait_recv()
        msg_f(l, e, x_peer).start()

    def ready(l, e):
        msg_c(l, e, c_peer).wait_recv()
        msg_f(l, e, xc_peer).wait_recv()

    def sent(l):
        for e in range(nc):
            msg_x(l, e, w).wait_send()
            msg_c(l, e, w).wait_send()
            msg_f(l, e, x_peer).wait_send()

    def product(l, e, tap):
        return jnp.dot(
            hids[l][span(e), :], wb[l, tap], preferred_element_type=jnp.float32
        )

    def msg_g(l, i):
        ref = pl.ds(0, reach[l] * CHUNK)
        return rdma(
            part_out.at[l, i, ref, :], part_in.at[l, i, ref, :],
            s_g.at[l, i], r_g.at[l, i], s + (1 if i == 0 else -1), w,
        )

    def tap_first(l, lo, hi):
        d = reach[l]
        cut = nc - d
        if lo < min(hi, cut):
            @pl.loop(lo, min(hi, cut))
            def _(e):
                acc[span(e + d), :] += product(l, e, 0)

        if max(lo, cut) < hi:
            @pl.loop(max(lo, cut), hi)
            def _(e):
                part_out[l, 0, span(e - cut), :] = product(l, e, 0).astype(jnp.bfloat16)

        if hi == nc:
            pl.when(has_next)(msg_g(l, 0).start)

    def tap_third(l, lo, hi):
        d = reach[l]
        if lo < d:
            @pl.loop(lo, min(hi, d))
            def _(e):
                part_out[l, 1, span(e), :] = product(l, e, TAPS - 1).astype(jnp.bfloat16)

            if hi >= d:
                pl.when(has_prev)(msg_g(l, 1).start)

        if max(lo, d) < hi:
            @pl.loop(max(lo, d), hi)
            def _(e):
                acc[span(e - d), :] += product(l, e, TAPS - 1)

    def neighbours(l):
        count = reach[l] * CHUNK
        for i, there, at in ((0, has_prev, 0), (1, has_next, rows - count)):
            @pl.when(there)
            def _():
                msg_g(l, i).wait_recv()
                acc[pl.ds(at, count), :] += part_in[l, i, pl.ds(0, count), :].astype(jnp.float32)

    def tap_middle(l, lo, hi):
        @pl.loop(lo, hi)
        def _(c):
            state = (acc[span(c), :] + product(l, c, 1)).astype(jnp.bfloat16)
            if l == 0:
                acc[span(c), :] = state.astype(jnp.float32)
                emit(1, c, state)
            else:
                out_ref[span(c), :] = state

    last = reach[1]
    groups = [(nc - last, nc)] + [(lo, min(lo + 2, nc - last)) for lo in range(0, nc - last, 2)]
    place = {c: (c + last) % nc for c in range(nc)}

    def events():
        out = []

        def put(when, go, *operands):
            out.append((when, functools.partial(go, *operands)))

        for l, base in ((0, 0.0), (1, 44.0)):
            ends = {}
            for i, tap in enumerate(ORDER):
                length = 21.0 if tap == LAST else 10.5
                at = base + 10.5 * i
                for k in range(1, lines):
                    when = at + length * k / (lines - 1)
                    put(when, weights_step, l, tap, k)
                    if k == max(1, lines - 2):
                        if i == 0:
                            put(when, weights_start, l, LAST)
                        if tap == LAST and l == 0:
                            put(when, weights_start, 1, ORDER[0])
                            put(when, weights_start, 1, ORDER[1])
                ends[tap] = at + length + (0.0 if tap == LAST else 6.0)
            here = [base + 1.0 + 36.8 * (i + 1) / nc for i in range(nc)]
            for i in range(nc):
                e = (i + nc - last) % nc
                put(here[i], forward, l, e)
                put(here[i] + 1.5, ready, l, e)
            put(ends[0], weights_finish, l, 0)
            put(ends[2], weights_finish, l, 2)
            for lo, hi in groups:
                come = here[place[hi - 1]]
                put(max(come + 1.6, ends[0] + 0.1), tap_first, l, lo, hi)
                put(max(come + 1.7, ends[2] + 0.1), tap_third, l, lo, hi)
            done = max(ends[LAST], here[-1] + 2.0) + 0.1
            put(done, weights_finish, l, LAST)
            put(done, neighbours, l)
            for i, (lo, hi) in enumerate(groups):
                put(done + 4.0 * i / len(groups), tap_middle, l, lo, hi)
        return [go for _, go in sorted(out, key=lambda entry: entry[0])]

    barrier = pltpu.get_barrier_semaphore()
    peers = [
        (True, y_peer, w), (True, s, x_peer), (True, s, c_peer),
        (up, s + 2, w), (down, s - 2, w), (has_next, s + 1, w), (has_prev, s - 1, w),
    ]
    expected = 3
    for there, ds, dw in peers:
        def greet(ds=ds, dw=dw):
            pl.semaphore_signal(
                barrier, inc=1, device_id=(ds, dw), device_id_type=pl.DeviceIdType.MESH
            )

        if there is True:
            greet()
        else:
            pl.when(there)(greet)
            expected = expected + there.astype(jnp.int32)
    wb[0, :, krows(z, y), :] = w1_ref[...]
    wb[1, :, krows(z, y), :] = w2_ref[...]
    pl.semaphore_wait(barrier, expected)

    weights_start(0, ORDER[0])
    weights_start(0, ORDER[1])

    @pl.loop(0, nc)
    def _(i):
        c = lax.rem(i + nc - last, nc)
        state = x_ref[span(c), :]
        acc[span(c), :] = state.astype(jnp.float32)
        emit(0, c, state)

    for go in events():
        go()

    for l in range(2):
        sent(l)
        weights_drain(l)
        pl.when(has_next)(msg_g(l, 0).wait_send)
        pl.when(has_prev)(msg_g(l, 1).wait_send)


def shards(n, m, x, s1, b1, w1, s2, b2, w2):
    rows, cols = x.shape
    channels = m * cols
    lines = n // 2
    dma = pltpu.SemaphoreType.DMA
    vmem = pl.BlockSpec(memory_space=pltpu.VMEM)
    return pl.pallas_call(
        functools.partial(tower_kernel, n, m),
        out_shape=jax.ShapeDtypeStruct((rows, cols), jnp.bfloat16),
        in_specs=[vmem] * 7,
        out_specs=vmem,
        scratch_shapes=[
            pltpu.VMEM((rows, channels), jnp.bfloat16),
            pltpu.VMEM((rows, channels), jnp.bfloat16),
            pltpu.VMEM((2, TAPS, channels, cols), jnp.bfloat16),
            pltpu.VMEM((rows, cols), jnp.float32),
            pltpu.VMEM((2, 2, DILATION_SECOND, cols), jnp.bfloat16),
            pltpu.VMEM((2, 2, DILATION_SECOND, cols), jnp.bfloat16),
            dma((2, 2)), dma((2, 2)),
            dma((2, 2 * TAPS, lines)), dma((2 * TAPS, lines)),
            dma((2, 2, lines)), dma((2, lines)),
            dma((2 * TAPS, lines)), dma((2 * TAPS, lines)),
        ] + [dma((2, rows // CHUNK))] * 6,
        compiler_params=pltpu.CompilerParams(
            collective_id=0, has_side_effects=True, vmem_limit_bytes=56 * 1024 * 1024
        ),
        cost_estimate=pl.CostEstimate(
            flops=4 * TAPS * rows * channels * cols,
            bytes_accessed=4 * rows * cols + 4 * TAPS * w1.shape[1] * cols,
            transcendentals=2 * rows * cols,
        ),
    )(x, s1, b1, w1, s2, b2, w2)


def solution(mesh):
    placed = (
        P("seq", "wt"),
        P("wt"),
        P("wt"),
        P(None, "seq", "wt"),
        P("wt"),
        P("wt"),
        P(None, "seq", "wt"),
    )
    n, m = mesh.shape["seq"], mesh.shape["wt"]
    return jax.shard_map(
        functools.partial(shards, n, m), mesh=mesh, in_specs=placed,
        out_specs=P("seq", "wt"), check_vma=False,
    )
```

```python
import functools

import jax
import jax.numpy as jnp
from jax import lax
from jax.experimental import pallas as pl
from jax.experimental.pallas import tpu as pltpu
from jax.sharding import PartitionSpec as P

DILATION_FIRST = 256
DILATION_SECOND = 512
CHUNK = 256
TAPS = 3
ORDER = (0, 2, 1)
LAST = ORDER[-1]


def tower_kernel(
    n, m, x_ref, s1_ref, b1_ref, w1_ref, s2_ref, b2_ref, w2_ref, out_ref,
    hid1, hid2, wb, acc, part_out, part_in, s_g, r_g,
    s_p, r_p, s_q, r_q, s_y, r_y, s_x, r_x, s_c, r_c, s_f, r_f,
):
    s = lax.axis_index("seq")
    w = lax.axis_index("wt")
    lines = n // 2
    z, y = s // 2, lax.rem(s, 2)
    x_peer = lax.rem(w + m // 2, m)
    c_peer = w + 1 - 2 * lax.rem(w, 2)
    xc_peer = lax.rem(c_peer + m // 2, m)
    y_peer = s + 1 - 2 * y
    rows, cols = x_ref.shape
    kr = w1_ref.shape[1]
    nc = rows // CHUNK
    reach = (DILATION_FIRST // CHUNK, DILATION_SECOND // CHUNK)
    hids = (hid1, hid2)
    scales = (s1_ref, s2_ref)
    shifts = (b1_ref, b2_ref)
    has_prev, has_next = s > 0, s < n - 1
    up, down = z < lines - 1, z > 0
    steps = ((1, up), (-1, down))

    def rdma(src, dst, ss, rs, ds, dw):
        return pltpu.make_async_remote_copy(
            src_ref=src, dst_ref=dst, send_sem=ss, recv_sem=rs,
            device_id=(ds, dw), device_id_type=pl.DeviceIdType.MESH,
        )

    def span(e):
        return pl.ds(pl.multiple_of(e * CHUNK, CHUNK), CHUNK)

    def lane(j):
        return pl.ds(pl.multiple_of(j * cols, cols), cols)

    def krows(zz, yy, lo=0, hi=None):
        hi = kr if hi is None else hi
        return pl.ds(pl.multiple_of((zz * 2 + yy) * kr + lo, 16), hi - lo)

    share = (kr // 32 * 16, kr // 32 * 16)

    def msg_p(l, tap, zz, d):
        ref = wb.at[l, tap, krows(zz, y), :]
        i, j = (0 if d > 0 else 1), l * TAPS + tap
        return rdma(ref, ref, s_p.at[i, j, zz], r_p.at[j, zz], s + 2 * d, w)

    def msg_q(l, zz, d):
        ref = wb.at[l, LAST, krows(zz, 1 - y, share[l], kr), :]
        i = 0 if d > 0 else 1
        return rdma(ref, ref, s_q.at[i, l, zz], r_q.at[l, zz], s + 2 * d, w)

    def msg_y(l, tap, zz, yy, whole=False):
        part = share[l] if tap == LAST and not whole else kr
        ref = wb.at[l, tap, krows(zz, yy, 0, part), :]
        j = l * TAPS + tap
        return rdma(ref, ref, s_y.at[j, zz], r_y.at[j, zz], y_peer, w)

    def weights_start(l, tap):
        if tap == ORDER[1]:
            msg_y(l, LAST, z, y, True).start()
        if tap == LAST:
            msg_y(l, LAST, z, 1 - y, True).wait_recv()
        else:
            msg_y(l, tap, z, y).start()
        for d, there in steps:
            @pl.when(there)
            def _():
                msg_p(l, tap, z, d).start()
                if tap == LAST:
                    msg_q(l, z, d).start()

    def weights_step(l, tap, k):
        low = z < lines // 2
        pl.when(low)(lambda: relay(l, tap, k, steps[::-1]))
        pl.when(jnp.logical_not(low))(lambda: relay(l, tap, k, steps))

    def relay(l, tap, k, ways):
        for d, there in ways:
            zz = z - d * k

            @pl.when(jnp.logical_and(zz >= 0, zz < lines))
            def _():
                msg_p(l, tap, zz, d).wait_recv()
                pl.when(there)(msg_p(l, tap, zz, d).start)
                if tap == LAST:
                    msg_q(l, zz, d).wait_recv()
                    pl.when(there)(msg_q(l, zz, d).start)
                if tap != LAST or share[l]:
                    msg_y(l, tap, zz, y).start()

    def weights_finish(l, tap):
        if tap == LAST and not share[l]:
            return
        if tap != LAST:
            msg_y(l, tap, z, 1 - y).wait_recv()
        for k in range(1, lines):
            for d in (1, -1):
                zz = z - d * k
                pl.when(jnp.logical_and(zz >= 0, zz < lines))(
                    msg_y(l, tap, zz, 1 - y).wait_recv
                )

    def weights_drain(l):
        for tap in range(TAPS):
            msg_y(l, tap, z, y, True).wait_send()
            for k in range(lines):
                for d, there in steps:
                    zz = z - d * k

                    @pl.when(jnp.logical_and(zz >= 0, zz < lines))
                    def _():
                        if k and (tap != LAST or share[l]):
                            msg_y(l, tap, zz, y).wait_send()

                        @pl.when(there)
                        def _():
                            msg_p(l, tap, zz, d).wait_send()
                            if tap == LAST:
                                msg_q(l, zz, d).wait_send()

    def msg_x(l, e, j):
        ref = hids[l].at[span(e), lane(j)]
        return rdma(ref, ref, s_x.at[l, e], r_x.at[l, e], s, x_peer)

    def msg_c(l, e, j):
        ref = hids[l].at[span(e), lane(j)]
        return rdma(ref, ref, s_c.at[l, e], r_c.at[l, e], s, c_peer)

    def msg_f(l, e, j):
        ref = hids[l].at[span(e), lane(j)]
        return rdma(ref, ref, s_f.at[l, e], r_f.at[l, e], s, c_peer)

    def emit(l, c, state):
        value = state.astype(jnp.float32) * scales[l][...][None, :] + shifts[l][...][None, :]
        hids[l][span(c), lane(w)] = jax.nn.gelu(value, approximate=True).astype(jnp.bfloat16)
        msg_x(l, c, w).start()
        msg_c(l, c, w).start()

    def forward(l, e):
        msg_x(l, e, x_peer).wait_recv()
        msg_f(l, e, x_peer).start()

    def ready(l, e):
        msg_c(l, e, c_peer).wait_recv()
        msg_f(l, e, xc_peer).wait_recv()

    def sent(l):
        for e in range(nc):
            msg_x(l, e, w).wait_send()
            msg_c(l, e, w).wait_send()
            msg_f(l, e, x_peer).wait_send()

    def product(l, e, tap):
        return jnp.dot(
            hids[l][span(e), :], wb[l, tap], preferred_element_type=jnp.float32
        )

    def msg_g(l, i):
        ref = pl.ds(0, reach[l] * CHUNK)
        return rdma(
            part_out.at[l, i, ref, :], part_in.at[l, i, ref, :],
            s_g.at[l, i], r_g.at[l, i], s + (1 if i == 0 else -1), w,
        )

    def tap_first(l, lo, hi):
        d = reach[l]
        cut = nc - d
        if lo < min(hi, cut):
            @pl.loop(lo, min(hi, cut))
            def _(e):
                acc[span(e + d), :] += product(l, e, 0)

        if max(lo, cut) < hi:
            @pl.loop(max(lo, cut), hi)
            def _(e):
                part_out[l, 0, span(e - cut), :] = product(l, e, 0).astype(jnp.bfloat16)

        if hi == nc:
            pl.when(has_next)(msg_g(l, 0).start)

    def tap_third(l, lo, hi):
        d = reach[l]
        if lo < d:
            @pl.loop(lo, min(hi, d))
            def _(e):
                part_out[l, 1, span(e), :] = product(l, e, TAPS - 1).astype(jnp.bfloat16)

            if hi >= d:
                pl.when(has_prev)(msg_g(l, 1).start)

        if max(lo, d) < hi:
            @pl.loop(max(lo, d), hi)
            def _(e):
                acc[span(e - d), :] += product(l, e, TAPS - 1)

    def neighbours(l):
        count = reach[l] * CHUNK
        for i, there, at in ((0, has_prev, 0), (1, has_next, rows - count)):
            @pl.when(there)
            def _():
                msg_g(l, i).wait_recv()
                acc[pl.ds(at, count), :] += part_in[l, i, pl.ds(0, count), :].astype(jnp.float32)

    def tap_middle(l, lo, hi):
        @pl.loop(lo, hi)
        def _(c):
            state = (acc[span(c), :] + product(l, c, 1)).astype(jnp.bfloat16)
            if l == 0:
                acc[span(c), :] = state.astype(jnp.float32)
                emit(1, c, state)
            else:
                out_ref[span(c), :] = state

    last = reach[1]
    groups = [(nc - last, nc)] + [(lo, min(lo + 2, nc - last)) for lo in range(0, nc - last, 2)]
    place = {c: (c + last) % nc for c in range(nc)}

    def events():
        out = []

        def put(when, go, *operands):
            out.append((when, functools.partial(go, *operands)))

        for l, base in ((0, 0.0), (1, 44.0)):
            ends = {}
            for i, tap in enumerate(ORDER):
                length = 21.0 if tap == LAST else 10.5
                at = base + 10.5 * i
                for k in range(1, lines):
                    when = at + length * k / (lines - 1)
                    put(when, weights_step, l, tap, k)
                    if k == max(1, lines - 2):
                        if i == 0:
                            put(when, weights_start, l, LAST)
                        if tap == LAST and l == 0:
                            put(when, weights_start, 1, ORDER[0])
                            put(when, weights_start, 1, ORDER[1])
                ends[tap] = at + length + (0.0 if tap == LAST else 6.0)
            here = [base + 1.0 + 36.8 * (i + 1) / nc for i in range(nc)]
            for i in range(nc):
                e = (i + nc - last) % nc
                put(here[i], forward, l, e)
                put(here[i] + 1.5, ready, l, e)
            put(ends[0], weights_finish, l, 0)
            put(ends[2], weights_finish, l, 2)
            for lo, hi in groups:
                come = here[place[hi - 1]]
                put(max(come + 1.6, ends[0] + 0.1), tap_first, l, lo, hi)
                put(max(come + 1.7, ends[2] + 0.1), tap_third, l, lo, hi)
            done = max(ends[LAST], here[-1] + 2.0) + 0.1
            put(done, weights_finish, l, LAST)
            put(done, neighbours, l)
            for i, (lo, hi) in enumerate(groups):
                put(done + 4.0 * i / len(groups), tap_middle, l, lo, hi)
        return [go for _, go in sorted(out, key=lambda entry: entry[0])]

    barrier = pltpu.get_barrier_semaphore()
    peers = [
        (True, y_peer, w), (True, s, x_peer), (True, s, c_peer),
        (up, s + 2, w), (down, s - 2, w), (has_next, s + 1, w), (has_prev, s - 1, w),
    ]
    expected = 3
    for there, ds, dw in peers:
        def greet(ds=ds, dw=dw):
            pl.semaphore_signal(
                barrier, inc=1, device_id=(ds, dw), device_id_type=pl.DeviceIdType.MESH
            )

        if there is True:
            greet()
        else:
            pl.when(there)(greet)
            expected = expected + there.astype(jnp.int32)
    wb[0, :, krows(z, y), :] = w1_ref[...]
    wb[1, :, krows(z, y), :] = w2_ref[...]
    pl.semaphore_wait(barrier, expected)

    weights_start(0, ORDER[0])
    weights_start(0, ORDER[1])

    @pl.loop(0, nc)
    def _(i):
        c = lax.rem(i + nc - last, nc)
        state = x_ref[span(c), :]
        acc[span(c), :] = state.astype(jnp.float32)
        emit(0, c, state)

    for go in events():
        go()

    for l in range(2):
        sent(l)
        weights_drain(l)
        pl.when(has_next)(msg_g(l, 0).wait_send)
        pl.when(has_prev)(msg_g(l, 1).wait_send)


def shards(n, m, x, s1, b1, w1, s2, b2, w2):
    rows, cols = x.shape
    channels = m * cols
    lines = n // 2
    dma = pltpu.SemaphoreType.DMA
    vmem = pl.BlockSpec(memory_space=pltpu.VMEM)
    return pl.pallas_call(
        functools.partial(tower_kernel, n, m),
        out_shape=jax.ShapeDtypeStruct((rows, cols), jnp.bfloat16),
        in_specs=[vmem] * 7,
        out_specs=vmem,
        scratch_shapes=[
            pltpu.VMEM((rows, channels), jnp.bfloat16),
            pltpu.VMEM((rows, channels), jnp.bfloat16),
            pltpu.VMEM((2, TAPS, channels, cols), jnp.bfloat16),
            pltpu.VMEM((rows, cols), jnp.float32),
            pltpu.VMEM((2, 2, DILATION_SECOND, cols), jnp.bfloat16),
            pltpu.VMEM((2, 2, DILATION_SECOND, cols), jnp.bfloat16),
            dma((2, 2)), dma((2, 2)),
            dma((2, 2 * TAPS, lines)), dma((2 * TAPS, lines)),
            dma((2, 2, lines)), dma((2, lines)),
            dma((2 * TAPS, lines)), dma((2 * TAPS, lines)),
        ] + [dma((2, rows // CHUNK))] * 6,
        compiler_params=pltpu.CompilerParams(
            collective_id=0, has_side_effects=True, vmem_limit_bytes=56 * 1024 * 1024
        ),
        cost_estimate=pl.CostEstimate(
            flops=4 * TAPS * rows * channels * cols,
            bytes_accessed=4 * rows * cols + 4 * TAPS * w1.shape[1] * cols,
            transcendentals=2 * rows * cols,
        ),
    )(x, s1, b1, w1, s2, b2, w2)


def solution(mesh):
    placed = (
        P("seq", "wt"),
        P("wt"),
        P("wt"),
        P(None, "seq", "wt"),
        P("wt"),
        P("wt"),
        P(None, "seq", "wt"),
    )
    n, m = mesh.shape["seq"], mesh.shape["wt"]
    return jax.shard_map(
        functools.partial(shards, n, m), mesh=mesh, in_specs=placed,
        out_specs=P("seq", "wt"), check_vma=False,
    )
```
